256 devices in a mesh: seq: 8 (over z_hi, core), fsdp: 32 (over x, y, z_lo).
Axes of the slice: x: 4, y: 4, z: 8 (z_hi: 4, z_lo: 2; z = z_hi * 2 + z_lo), core: 2. Of those that a mesh axis runs over, the one named last changes fastest.
Arguments:
- tokens: bfloat16 [32, 2, 1024, 1024], P('fsdp', None, 'seq'), may hold values from -6 to 6
- proj: bfloat16 [1024, 3, 512], P('fsdp'), may hold values from -0.1875 to 0.1875
- state: float32 [32, 2, 3, 256, 512], P('fsdp'), may hold values from -0.375 to 0.375
- step_rates: float32 [32, 2, 1024], P('fsdp', None, 'seq'), may hold values from 0.00048828125 to 0.0048828125
- d_out: bfloat16 [32, 2, 1024, 512], P('fsdp', None, 'seq'), may hold values from -6 to 6
Outputs:
- d_tokens: bfloat16 [32, 2, 1024, 1024], P('fsdp', None, 'seq')
- d_state: float32 [32, 2, 3, 256, 512], P('fsdp', None, None, 'seq')
- d_proj: float32 [1024, 3, 512], P('fsdp')
The draws below stay inside these ranges and needn't reach their ends.
All inputs are finite; a program needn't handle non-finite values.
Results may differ from the reference program's by a relative error of at most 0.04.
Values may be sent and summed in bfloat16 or wider, within the bound.
No kernel may reach another device: no remote copies, remote signals or barrier semaphores. Data moves between devices by JAX's collectives and lax.ppermute only.
A program may use at most 128 MiB of HBM per device.

```python
import math
from functools import partial
import jax
import jax.numpy as jnp
from jax import lax

D = 1024
HEADS = 2
DH = 256
M = 512
TOK_DEV = 128
C = 1024
BATCH = 32
HD = 512
N_SEQ = 8


def raised(entries, key, source, target, blocks, factor):
    owner, partner = [(jnp.arange(entries.shape[position]) // (entries.shape[position] // blocks)).reshape([-1 if axis == position else 1 for axis in range(entries.ndim)]) for position in (source, target)]
    chosen = jax.random.permutation(key, blocks)[partner]
    strong = (owner == chosen) | (owner == (partner + blocks // 2) % blocks)
    return jnp.where(strong, factor * entries, entries)


def level_of(stream_key, dims, split, least, top_value):
    level = 1.0
    for dim, shards_of in split:
        draws = jax.random.uniform(jax.random.fold_in(jax.random.fold_in(stream_key, 6), dim), (shards_of,), jnp.float32, least / len(split), top_value / len(split))
        level = level * jnp.repeat(jnp.exp(draws), dims[dim] // shards_of).reshape((-1,) + (1,) * (len(dims) - 1 - dim))
    return level


def bell_draw(key, dims, scale, reach, cuts=(), held_as=jnp.bfloat16):
    loudness = level_of(key, dims, cuts, -0.22, 0.18) if cuts else 1.0
    drawn = jax.random.normal(key, dims, jnp.float32) * scale * loudness
    return jnp.minimum(jnp.maximum(drawn, -reach), reach).astype(held_as)


def gaussian_with(own_key, shape, spread, most, pieces, heavy, kind=jnp.bfloat16):
    entries = spread * jax.random.normal(own_key, shape, jnp.float32)
    if pieces:
        entries = entries * level_of(own_key, shape, pieces, -0.22, 0.18)
    return jnp.clip(raised(entries, jax.random.fold_in(own_key, 3), *heavy), -most, most).astype(kind)


def setup_inputs(seed: int = 0) -> dict:
    splits = jax.random.split(jax.random.key(seed), 6)
    tokens = gaussian_with(splits[0], (BATCH, 2, C, D), 1.0, 6.0, ((0, 32), (2, 8)), (0, 3, 32, 2.75))
    proj = bell_draw(splits[1], (D, 3, HD), D ** -0.5, 0.1875, ((0, 32),))
    state = bell_draw(splits[2], (BATCH, HEADS, 3, DH, M), DH ** -0.5, 0.375, ((0, 32),), jnp.float32)
    step_rates = jnp.clip(jnp.exp(math.log(0.0048828125) - 2.3025851 * jax.random.uniform(splits[3], (BATCH, HEADS, C), jnp.float32) ** level_of(splits[3], (BATCH, HEADS, C), ((0, 32), (2, 8)), -0.2, 0.2)), 0.00048828125, 0.0048828125)
    d_out = bell_draw(splits[4], (BATCH, 2, C, HD), 1.0, 6.0, ((0, 32), (2, 8)))
    return {"tokens": tokens, "proj": proj, "state": state, "step_rates": step_rates, "d_out": d_out}


HIGH = lax.Precision.HIGHEST
EPS = 1e-06

def unit_rows(values):
    return values * lax.rsqrt(lax.optimization_barrier(jnp.mean(values * values, axis=-1, keepdims=True)) + EPS)

def fast_apply(weights, inputs):
    gate_part = jnp.einsum('rhd,hdm->rhm', inputs, weights[:, 0], precision=HIGH)
    up_part = jnp.einsum('rhd,hdm->rhm', inputs, weights[:, 1], precision=HIGH)
    hidden = jax.nn.silu(gate_part) * up_part
    return jnp.einsum('rhm,hdm->rhd', hidden, weights[:, 2], precision=HIGH)

def update_term(learn_rate, weights, key_rows, values):

    def objective(current):
        return jnp.sum(fast_apply(current, unit_rows(key_rows)) * values * learn_rate[:, :, None])
    return jax.grad(objective)(weights)

def first_span(learn_rate, weights, queries, key_rows, values):
    return (fast_apply(weights, unit_rows(queries)), update_term(learn_rate, weights, key_rows, values))

def second_span(weights, queries):
    return fast_apply(weights, unit_rows(queries))

def reference(tokens, proj, state, step_rates, d_out):
    model_width = tokens.shape[-1]
    flat_proj = proj.reshape(model_width, 3 * HEADS * DH)

    def one_sequence(proj_sum, inputs):
        seq_tokens, start_state, seq_rates, seq_cot = inputs
        flat_tokens = seq_tokens.reshape(2 * C, model_width)
        packed = jnp.dot(flat_tokens, flat_proj, preferred_element_type=jnp.float32)
        rounded = lax.optimization_barrier(packed.astype(jnp.bfloat16))
        projected = rounded.astype(jnp.float32).reshape(2, N_SEQ, TOK_DEV, 3, HEADS, DH)
        cotangent = seq_cot.astype(jnp.float32).reshape(2, N_SEQ, TOK_DEV, HEADS, DH)
        block_rates = seq_rates.reshape(HEADS, N_SEQ, TOK_DEV).transpose(1, 2, 0)

        def update_block(block_data):
            key_rows, value_rows, learn_rate = block_data
            return update_term(learn_rate, start_state, key_rows, value_rows).astype(jnp.bfloat16)
        updates = lax.map(update_block, (projected[0, :, :, 1], projected[0, :, :, 2], block_rates))
        next_state = start_state + lax.optimization_barrier(jnp.sum(updates.astype(jnp.float32), axis=0))

        def late_block(block_data):
            query_rows, cot_rows = block_data
            _, pullback = jax.vjp(second_span, next_state, query_rows)
            grad_state, grad_query = pullback(cot_rows)
            return (grad_state.astype(jnp.bfloat16), grad_query)
        late_grads, late_queries = lax.map(late_block, (projected[1, :, :, 0], cotangent[1]))
        carried = lax.optimization_barrier(jnp.sum(late_grads.astype(jnp.float32), axis=0))

        def early_block(block_data):
            query_rows, key_rows, value_rows, learn_rate, cot_rows = block_data
            _, pullback = jax.vjp(partial(first_span, learn_rate), start_state, query_rows, key_rows, value_rows)
            grad_state, grad_query, grad_key, grad_value = pullback((cot_rows, carried))
            return (grad_state.astype(jnp.bfloat16), jnp.stack([grad_query, grad_key, grad_value], axis=1))
        early_grads, early_parts = lax.map(early_block, (projected[0, :, :, 0], projected[0, :, :, 1], projected[0, :, :, 2], block_rates, cotangent[0]))
        state_grad = carried + lax.optimization_barrier(jnp.sum(early_grads.astype(jnp.float32), axis=0))
        late_full = jnp.concatenate([late_queries[:, :, None], jnp.zeros_like(early_parts[:, :, 1:])], axis=2)
        grad_parts = jnp.stack([early_parts, late_full]).astype(jnp.bfloat16).reshape(2 * C, 3 * HEADS * DH)
        grad_tokens = lax.dot_general(grad_parts, flat_proj, (((1,), (1,)), ((), ())), preferred_element_type=jnp.float32).astype(jnp.bfloat16)
        proj_sum = proj_sum + lax.dot_general(flat_tokens, grad_parts, (((0,), (0,)), ((), ())), preferred_element_type=jnp.float32)
        return (proj_sum, (grad_tokens.reshape(2, C, model_width), state_grad))
    initial = jnp.zeros((model_width, 3 * HEADS * DH), jnp.float32)
    proj_sum, (grad_tokens, state_grads) = lax.scan(one_sequence, initial, (tokens, state, step_rates, d_out))
    return (grad_tokens, state_grads, proj_sum.reshape(proj.shape))
```

```python
from functools import partial

import jax
import jax.numpy as jnp
from jax import lax
from jax.experimental import pallas as pl
from jax.experimental.pallas import tpu as pltpu
from jax.sharding import PartitionSpec as P

EPS = 1e-06
BF = jnp.bfloat16
F32 = jnp.float32
CORES = 2


def dot_nn(a, b):
    return lax.dot_general(a, b, (((1,), (0,)), ((), ())), preferred_element_type=F32)


def dot_nt(a, b):
    return lax.dot_general(a, b, (((1,), (1,)), ((), ())), preferred_element_type=F32)


def dot_tn(a, b):
    return lax.dot_general(a, b, (((0,), (0,)), ((), ())), preferred_element_type=F32)


def inverse_rms(values):
    return lax.rsqrt(jnp.mean(values * values, axis=-1, keepdims=True) + EPS)


def unit_pull(grad, unit, scale):
    return scale * (grad - unit * jnp.mean(grad * unit, axis=-1, keepdims=True))


def as_column(row):
    count = row.shape[1]
    eye = lax.broadcasted_iota(jnp.int32, (count, count), 0) == lax.broadcasted_iota(
        jnp.int32, (count, count), 1
    )
    return jnp.sum(jnp.where(eye, row, 0.0), axis=1, keepdims=True)


def hidden_parts(unit, cot, weights):
    gate = dot_nn(unit, weights[0])
    up = dot_nn(unit, weights[1])
    back = dot_nn(cot, weights[2])
    sig = 0.5 * jnp.tanh(0.5 * gate) + 0.5
    act = gate * sig
    slope = sig + act * (1.0 - sig)
    return gate, up, back, sig, act, slope


def weight_terms(unit, cot, weights):
    gate, up, back, sig, act, slope = hidden_parts(unit, cot, weights)
    d_up = (back * act).astype(BF)
    d_gate = (back * up * slope).astype(BF)
    hidden = (act * up).astype(BF)
    return d_gate, d_up, hidden


def update_kernel(count, *refs):
    tok = refs[: 2 * count]
    proj, state, rates, cot0, cot0_mate = refs[2 * count : 2 * count + 5]
    next_ref, kv_ref, early_ref, dq_ref = refs[2 * count + 5 : 2 * count + 9]
    keys, w16, total = refs[2 * count + 9 :]
    rows = tok[0].shape[0]
    dim = state.shape[1]
    span = 2 * rows
    for part in range(3):
        w16[part] = state[part].astype(BF)
    weights = (w16[0], w16[1], w16[2])
    own = jnp.concatenate([tok[0][...], tok[1][...]], axis=0)
    query = dot_nn(own, proj[:, :dim]).astype(BF).astype(F32)
    scale = inverse_rms(query)
    unit = query * scale
    unit16 = unit.astype(BF)
    cot = jnp.concatenate([cot0[...], cot0_mate[...]], axis=0)
    d_gate, d_up, hidden = weight_terms(unit16, cot, weights)
    early_ref[0] = dot_tn(unit16, d_gate)
    early_ref[1] = dot_tn(unit16, d_up)
    early_ref[2] = dot_tn(cot, hidden)
    pulled = dot_nt(d_gate, weights[0]) + dot_nt(d_up, weights[1])
    dq_ref[...] = unit_pull(pulled, unit, scale).astype(BF)

    for block in range(count):
        both = jnp.concatenate([tok[2 * block][...], tok[2 * block + 1][...]], axis=0)
        keys[pl.ds(block * span, span), :] = dot_nn(both, proj[:, dim:]).astype(BF)
    kv_ref[...] = keys[pl.ds(0, span), :]
    for part in range(3):
        total[part] = state[part]

    def step(block, carry):
        pair = keys[pl.ds(pl.multiple_of(block * span, span), span), :].astype(F32)
        rate = jnp.concatenate(
            [as_column(rates[pl.ds(2 * block + half, 1), :]) for half in range(2)], axis=0
        )
        key = pair[:, :dim]
        unit16 = (key * inverse_rms(key)).astype(BF)
        cot = (pair[:, dim:] * rate).astype(BF)
        d_gate, d_up, hidden = weight_terms(unit16, cot, (w16[0], w16[1], w16[2]))
        total[0] += dot_tn(unit16, d_gate)
        total[1] += dot_tn(unit16, d_up)
        total[2] += dot_tn(cot, hidden)
        return carry

    lax.fori_loop(0, count, step, 0)
    for part in range(3):
        next_ref[part] = total[part].astype(BF)


def late_kernel(count, place, *refs):
    queries = refs[:count]
    cots = refs[count : 2 * count]
    (next_w, state, rates, kv, early, dq0, tok0, tok0_mate, tok1, tok1_mate) = refs[
        2 * count : 2 * count + 10
    ]
    (own_ref, share_ref, dproj_ref, g0_ref, g1_ref) = refs[2 * count + 10 : 2 * count + 15]
    w16, c16, units, total = refs[2 * count + 15 :]
    span, dim = kv.shape[0], state.shape[1]
    share = dim // count
    for part in range(3):
        w16[part] = state[part].astype(BF)
        total[part] = jnp.zeros_like(total[part])
    late = (next_w[0], next_w[1], next_w[2])
    for block in range(count):
        query = queries[block][...].astype(F32)
        scale = inverse_rms(query)
        unit = query * scale
        unit16 = unit.astype(BF)
        cot = cots[block][...]
        d_gate, d_up, hidden = weight_terms(unit16, cot, late)
        total[0] += dot_tn(unit16, d_gate)
        total[1] += dot_tn(unit16, d_up)
        total[2] += dot_tn(cot, hidden)
        if block == 0:
            pulled = dot_nt(d_gate, late[0]) + dot_nt(d_up, late[1])
            g1_ref[...] = unit_pull(pulled, unit, scale).astype(BF)
    for part in range(3):
        c16[part] = total[part].astype(BF)
    start = pl.multiple_of(place[0] * share, share)
    for part in range(3):
        own_ref[part] = total[part, pl.ds(start, share), :]

    pair = kv[...].astype(F32)
    key, value = pair[:, :dim], pair[:, dim:]
    rate = jnp.concatenate([as_column(rates[half : half + 1, :]) for half in range(2)], axis=0)
    scale = inverse_rms(key)
    unit = key * scale
    unit16 = unit.astype(BF)
    cot = (value * rate).astype(BF)
    gate, up, back, sig, act, slope = hidden_parts(unit16, cot, (w16[0], w16[1], w16[2]))
    curve = sig * (1.0 - sig) * (2.0 + gate * (1.0 - 2.0 * sig))
    gate_dot = dot_nn(unit16, c16[0])
    up_dot = dot_nn(unit16, c16[1])
    back_dot = dot_nn(cot, c16[2])
    d_up1 = (back * act).astype(BF)
    d_gate1 = (back * up * slope).astype(BF)
    hidden = (act * up).astype(BF)
    slope_dot = slope * gate_dot
    hidden_dot = (slope_dot * up + act * up_dot).astype(BF)
    d_gate = (back * (curve * gate_dot * up + slope * up_dot) + back_dot * slope * up).astype(BF)
    d_up = (back * slope_dot + back_dot * act).astype(BF)
    d_value = rate * (dot_nt(hidden_dot, w16[2]) + dot_nt(hidden, c16[2]))
    d_unit = (
        dot_nt(d_gate, w16[0])
        + dot_nt(d_up, w16[1])
        + dot_nt(d_gate1, c16[0])
        + dot_nt(d_up1, c16[1])
    )
    g0_ref[:, :dim] = dq0[...]
    g0_ref[:, dim : 2 * dim] = unit_pull(d_unit, unit, scale).astype(BF)
    g0_ref[:, 2 * dim :] = d_value.astype(BF)
    total[0] = early[0] + dot_tn(unit16, d_gate)
    total[1] = early[1] + dot_tn(unit16, d_up)
    total[2] = early[2] + dot_tn(cot, hidden_dot)
    for other in range(count):
        at = lax.rem(place[0] + other, count)
        at = pl.multiple_of(at * share, share)
        for part in range(3):
            share_ref[other, part] = total[part, pl.ds(at, share), :].astype(BF)

    width = tok0.shape[1]
    columns = 256

    def project(step, carry):
        at = pl.ds(pl.multiple_of(step * columns, columns), columns)
        first = jnp.concatenate([tok0[:, at], tok0_mate[:, at]], axis=0)
        second = jnp.concatenate([tok1[:, at], tok1_mate[:, at]], axis=0)
        out = dot_tn(first, g0_ref[...])
        extra = dot_tn(second, g1_ref[...])
        dproj_ref[at, :dim] = (out[:, :dim] + extra).astype(BF)
        dproj_ref[at, dim:] = out[:, dim:].astype(BF)
        return carry

    lax.fori_loop(0, width // columns, project, 0)


VMEM = pl.BlockSpec(memory_space=pltpu.VMEM)
SMEM = pl.BlockSpec(memory_space=pltpu.SMEM)


def on_device(groups, tokens, proj, state, step_rates, d_out):
    rows, width = tokens.shape[2:]
    heads, _, dim, hid = state.shape[1:]
    owned = proj.shape[0]
    peers = groups
    span = CORES * rows
    spot = lax.axis_index("seq")
    core = lax.rem(spot, CORES)
    place = spot // CORES

    def to_mate(value):
        return lax.ppermute(
            value, "seq", [(i, (i // CORES) * CORES + (i + 1) % CORES) for i in range(groups * CORES)]
        )

    def along(value, hop):
        return lax.ppermute(
            value,
            "seq",
            [(i, ((i // CORES + hop) % groups) * CORES + i % CORES) for i in range(groups * CORES)],
        )

    hops = range(1, groups)

    def mine(value):
        half = value.shape[-1] // CORES
        return jnp.where(core == 0, value[..., :half], value[..., half:])

    def other(value):
        half = value.shape[-1] // CORES
        return jnp.where(core == 0, value[..., half:], value[..., :half])

    tok = tokens[0]
    tok_mate = to_mate(tok)
    pieces = [tok[0], tok_mate[0]]
    far = [along(tok[0], hop) for hop in hops]
    for item in far:
        pieces += [item, to_mate(item)]
    cot = mine(d_out[0])
    cot_mate = to_mate(other(d_out[0]))
    cot1 = jnp.concatenate([cot[1], cot_mate[1]], axis=0)
    cots = [cot1] + [along(cot1, hop) for hop in hops]
    rate = step_rates[0]
    all_rates = jnp.stack([rate] + [along(rate, hop) for hop in hops])
    rate_mine = jnp.where(core == 0, all_rates[:, 0], all_rates[:, 1])
    rate_mate = to_mate(jnp.where(core == 0, all_rates[:, 1], all_rates[:, 0]))
    rates = jnp.stack([rate_mine, rate_mate], axis=1).reshape(groups * CORES, rows)

    proj_mine = mine(proj).reshape(1, owned, 3 * dim)
    devices = lax.axis_size("fsdp")
    whole = lax.all_to_all(
        jnp.broadcast_to(proj_mine, (devices, owned, 3 * dim)), "fsdp", 0, 0, tiled=True
    ).reshape(devices * owned, 3 * dim)
    own_state = jnp.where(core == 0, state[0, 0], state[0, 1])

    second = jnp.concatenate([tok[1], tok_mate[1]], axis=0)
    query1 = jnp.dot(second, whole[:, :dim], preferred_element_type=F32).astype(BF)
    queries = [query1] + [along(query1, hop) for hop in hops]

    shape = jax.ShapeDtypeStruct
    params = pltpu.CompilerParams(vmem_limit_bytes=56 * 2**20)
    next16, kv, early, dq0 = pl.pallas_call(
        partial(update_kernel, groups),
        out_shape=(
            shape((3, dim, hid), BF),
            shape((span, 2 * dim), BF),
            shape((3, dim, hid), F32),
            shape((span, dim), BF),
        ),
        in_specs=[VMEM] * (2 * groups + 5),
        out_specs=(VMEM,) * 4,
        scratch_shapes=[
            pltpu.VMEM((groups * span, 2 * dim), BF),
            pltpu.VMEM((3, dim, hid), BF),
            pltpu.VMEM((3, dim, hid), F32),
        ],
        compiler_params=params,
        name="update",
    )(*pieces, whole, own_state, rates, cot[0], cot_mate[0])

    share = dim // groups
    carried, shares, dproj, grads0, grads1 = pl.pallas_call(
        partial(late_kernel, groups),
        out_shape=(
            shape((3, share, hid), F32),
            shape((groups, 3, share, hid), BF),
            shape((width, 3 * dim), BF),
            shape((span, 3 * dim), BF),
            shape((span, dim), BF),
        ),
        in_specs=[SMEM] + [VMEM] * (2 * groups + 10),
        out_specs=(VMEM,) * 5,
        scratch_shapes=[
            pltpu.VMEM((3, dim, hid), BF),
            pltpu.VMEM((3, dim, hid), BF),
            pltpu.VMEM((8, 128), F32),
            pltpu.VMEM((3, dim, hid), F32),
        ],
        compiler_params=params,
        name="late",
    )(
        place.reshape(1).astype(jnp.int32),
        *queries,
        *cots,
        next16,
        own_state,
        rates,
        kv,
        early,
        dq0,
        tok[0],
        tok_mate[0],
        tok[1],
        tok_mate[1],
    )

    swapped = lax.all_to_all(dproj.reshape(devices, owned, 3 * dim), "fsdp", 0, 0, tiled=True)
    owner = jnp.sum(swapped.astype(F32), axis=0).astype(BF)
    owner_all = owner.astype(F32)
    for hop in hops:
        owner_all = owner_all + along(owner, hop).astype(F32)
    owner_mate = to_mate(owner_all)
    owner_all = owner_all.reshape(owned, 3, dim)
    owner_mate = owner_mate.reshape(owned, 3, dim)
    d_proj = jnp.where(
        core == 0,
        jnp.concatenate([owner_all, owner_mate], axis=-1),
        jnp.concatenate([owner_mate, owner_all], axis=-1),
    )

    summed = carried + shares[0].astype(F32)
    for hop in hops:
        summed = summed + along(shares[hop], hop).astype(F32)
    half = share // CORES
    keep = jnp.where(core == 0, summed[:, :half], summed[:, half:])
    give = jnp.where(core == 0, summed[:, half:], summed[:, :half])
    got = to_mate(give)
    d_state = jnp.where(core == 0, jnp.stack([keep, got]), jnp.stack([got, keep]))[None]

    part0 = lax.dot_general(
        grads0, whole, (((1,), (1,)), ((), ())), preferred_element_type=F32
    )
    part1 = lax.dot_general(
        grads1, whole[:, :dim], (((1,), (1,)), ((), ())), preferred_element_type=F32
    )
    part = jnp.stack([part0, part1])
    from_mate = to_mate(part[:, rows:].astype(BF))
    d_tokens = (part[:, :rows] + from_mate.astype(F32)).astype(BF)[None]
    return (d_tokens, d_state, d_proj)


def solution(mesh):
    groups = mesh.shape["seq"] // CORES
    placed = (
        P("fsdp", None, "seq", None),
        P("fsdp", None, None),
        P("fsdp", None, None, None, None),
        P("fsdp", None, "seq"),
        P("fsdp", None, "seq", None),
    )
    return jax.shard_map(
        partial(on_device, groups),
        mesh=mesh,
        in_specs=placed,
        out_specs=(
            P("fsdp", None, "seq", None),
            P("fsdp", None, None, "seq", None),
            P("fsdp", None, None),
        ),
        check_vma=False,
    )
```

```python
from functools import partial

import jax
import jax.numpy as jnp
from jax import lax
from jax.experimental import pallas as pl
from jax.experimental.pallas import tpu as pltpu
from jax.sharding import PartitionSpec as P

EPS = 1e-06
BF = jnp.bfloat16
F32 = jnp.float32
CORES = 2


def dot_nn(a, b):
    return lax.dot_general(a, b, (((1,), (0,)), ((), ())), preferred_element_type=F32)


def dot_nt(a, b):
    return lax.dot_general(a, b, (((1,), (1,)), ((), ())), preferred_element_type=F32)


def dot_tn(a, b):
    return lax.dot_general(a, b, (((0,), (0,)), ((), ())), preferred_element_type=F32)


def inverse_rms(values):
    return lax.rsqrt(jnp.mean(values * values, axis=-1, keepdims=True) + EPS)


def unit_pull(grad, unit, scale):
    return scale * (grad - unit * jnp.mean(grad * unit, axis=-1, keepdims=True))


def as_column(row):
    count = row.shape[1]
    eye = lax.broadcasted_iota(jnp.int32, (count, count), 0) == lax.broadcasted_iota(
        jnp.int32, (count, count), 1
    )
    return jnp.sum(jnp.where(eye, row, 0.0), axis=1, keepdims=True)


def hidden_parts(unit, cot, weights):
    gate = dot_nn(unit, weights[0])
    up = dot_nn(unit, weights[1])
    back = dot_nn(cot, weights[2])
    sig = 0.5 * jnp.tanh(0.5 * gate) + 0.5
    act = gate * sig
    slope = sig + act * (1.0 - sig)
    return gate, up, back, sig, act, slope


def weight_terms(unit, cot, weights):
    gate, up, back, sig, act, slope = hidden_parts(unit, cot, weights)
    d_up = (back * act).astype(BF)
    d_gate = (back * up * slope).astype(BF)
    hidden = (act * up).astype(BF)
    return d_gate, d_up, hidden


def piece_refs(refs, count):
    pieces = []
    for ref in refs[: 2 * (count - 1)]:
        half = ref.shape[1] // 2
        pieces.append((ref.at[:, :half], ref.at[:, half:]))
    for low, high in zip(refs[2 * (count - 1) :: 2], refs[2 * (count - 1) + 1 :: 2]):
        pieces.append((low, high))
    return pieces


def piece_rate(piece, rows, head):
    low, width = piece[0], rows
    row = rows
    line = low[row : row + 16, :].astype(F32)
    halves = []
    for level in range(2):
        pick = line[0:1, level * CORES * width : (level * CORES + 1) * width]
        rest = line[0:1, (level * CORES + 1) * width : (level + 1) * CORES * width]
        halves.append(jnp.where(head == 0, pick, rest))
    return as_column(halves[0] + halves[1])


def early_kernel(whole, state, tok, tok_mate, cot, cot_mate, early_ref, dq_ref):
    dim = state.shape[1]
    w1, w3, w2 = (state[part].astype(BF) for part in range(3))
    own = jnp.concatenate([tok[...], tok_mate[...]], axis=0)
    query = dot_nn(own, whole[:, :dim]).astype(BF).astype(F32)
    scale = inverse_rms(query)
    unit = query * scale
    unit16 = unit.astype(BF)
    cots = jnp.concatenate([cot[...], cot_mate[...]], axis=0)
    d_gate, d_up, hidden = weight_terms(unit16, cots, (w1, w3, w2))
    early_ref[0] = dot_tn(unit16, d_gate)
    early_ref[1] = dot_tn(unit16, d_up)
    early_ref[2] = dot_tn(cots, hidden)
    pulled = dot_nt(d_gate, w1) + dot_nt(d_up, w3)
    dq_ref[...] = unit_pull(pulled, unit, scale).astype(BF)


def update_kernel(count, rows, head_ref, *refs):
    refs = list(refs)
    pieces = piece_refs(refs[: 2 * count + 2], count)
    whole, state, next_ref, kv_ref, rate_ref, keys, w16, total = refs[2 * count + 2 :]
    dim = state.shape[1]
    half = whole.shape[0] // 2
    head = head_ref[0]
    for part in range(3):
        w16[part] = state[part].astype(BF)
        total[part] = state[part]
    for index, piece in enumerate(pieces):
        out = dot_nn(piece[0][:rows, :], whole[:half, dim:])
        out = out + dot_nn(piece[1][:rows, :], whole[half:, dim:])
        keys[index * rows : (index + 1) * rows, :] = out.astype(BF)
        rate_ref[index * rows : (index + 1) * rows, :] = jnp.broadcast_to(
            piece_rate(piece, rows, head), (rows, rate_ref.shape[1])
        )
    span = CORES * rows
    kv_ref[...] = keys[:span, :]

    def step(block, carry):
        at = pl.ds(pl.multiple_of(block * span, span), span)
        pair = keys[at, :].astype(F32)
        rate = rate_ref[at, :1]
        key = pair[:, :dim]
        unit16 = (key * inverse_rms(key)).astype(BF)
        cot = (pair[:, dim:] * rate).astype(BF)
        d_gate, d_up, hidden = weight_terms(unit16, cot, (w16[0], w16[1], w16[2]))
        total[0] += dot_tn(unit16, d_gate)
        total[1] += dot_tn(unit16, d_up)
        total[2] += dot_tn(cot, hidden)
        return carry

    lax.fori_loop(0, count, step, 0)
    for part in range(3):
        next_ref[part] = total[part].astype(BF)


def late_kernel(count, rows, place, *refs):
    refs = list(refs)
    dim = refs[count + 2].shape[1]
    queries = [ref.at[:, :dim] for ref in refs[: count - 1]] + [refs[count - 1]]
    cots = [ref.at[:, dim:] for ref in refs[: count - 1]] + [refs[count]]
    (next_w, state, rates, kv, early, dq0, tok0, tok0_mate, tok1, tok1_mate) = refs[
        count + 1 : count + 11
    ]
    (own_ref, share_ref, dproj_ref, g0_ref, g1_ref) = refs[count + 11 : count + 16]
    w16, c16, total = refs[count + 16 :]
    span, dim = kv.shape[0], state.shape[1]
    share = dim // count
    for part in range(3):
        w16[part] = state[part].astype(BF)
        total[part] = jnp.zeros_like(total[part])
    late = (next_w[0], next_w[1], next_w[2])
    for block in range(count):
        query = queries[block][...].astype(F32)
        scale = inverse_rms(query)
        unit = query * scale
        unit16 = unit.astype(BF)
        cot = cots[block][...]
        d_gate, d_up, hidden = weight_terms(unit16, cot, late)
        total[0] += dot_tn(unit16, d_gate)
        total[1] += dot_tn(unit16, d_up)
        total[2] += dot_tn(cot, hidden)
        if block == 0:
            pulled = dot_nt(d_gate, late[0]) + dot_nt(d_up, late[1])
            g1_ref[...] = unit_pull(pulled, unit, scale).astype(BF)
    for part in range(3):
        c16[part] = total[part].astype(BF)
    start = pl.multiple_of(place[0] * share, share)
    for part in range(3):
        own_ref[part] = total[part, pl.ds(start, share), :]

    pair = kv[...].astype(F32)
    key, value = pair[:, :dim], pair[:, dim:]
    rate = rates[:span, :1]
    scale = inverse_rms(key)
    unit = key * scale
    unit16 = unit.astype(BF)
    cot = (value * rate).astype(BF)
    gate, up, back, sig, act, slope = hidden_parts(unit16, cot, (w16[0], w16[1], w16[2]))
    curve = sig * (1.0 - sig) * (2.0 + gate * (1.0 - 2.0 * sig))
    gate_dot = dot_nn(unit16, c16[0])
    up_dot = dot_nn(unit16, c16[1])
    back_dot = dot_nn(cot, c16[2])
    d_up1 = (back * act).astype(BF)
    d_gate1 = (back * up * slope).astype(BF)
    hidden = (act * up).astype(BF)
    slope_dot = slope * gate_dot
    hidden_dot = (slope_dot * up + act * up_dot).astype(BF)
    d_gate = (back * (curve * gate_dot * up + slope * up_dot) + back_dot * slope * up).astype(BF)
    d_up = (back * slope_dot + back_dot * act).astype(BF)
    d_value = rate * (dot_nt(hidden_dot, w16[2]) + dot_nt(hidden, c16[2]))
    d_unit = (
        dot_nt(d_gate, w16[0])
        + dot_nt(d_up, w16[1])
        + dot_nt(d_gate1, c16[0])
        + dot_nt(d_up1, c16[1])
    )
    g0_ref[:, :dim] = dq0[...]
    g0_ref[:, dim : 2 * dim] = unit_pull(d_unit, unit, scale).astype(BF)
    g0_ref[:, 2 * dim :] = d_value.astype(BF)
    total[0] = early[0] + dot_tn(unit16, d_gate)
    total[1] = early[1] + dot_tn(unit16, d_up)
    total[2] = early[2] + dot_tn(cot, hidden_dot)
    for other in range(count):
        at = lax.rem(place[0] + other, count)
        at = pl.multiple_of(at * share, share)
        for part in range(3):
            share_ref[other, part] = total[part, pl.ds(at, share), :].astype(BF)

    width = tok0.shape[1]
    columns = 256

    def project(step, carry):
        at = pl.ds(pl.multiple_of(step * columns, columns), columns)
        first = jnp.concatenate([tok0[:rows, at], tok0_mate[:rows, at]], axis=0)
        second = jnp.concatenate([tok1[:, at], tok1_mate[:, at]], axis=0)
        out = dot_tn(first, g0_ref[...])
        extra = dot_tn(second, g1_ref[...])
        dproj_ref[at, :dim] = (out[:, :dim] + extra).astype(BF)
        dproj_ref[at, dim:] = out[:, dim:].astype(BF)
        return carry

    lax.fori_loop(0, width // columns, project, 0)


VMEM = pl.BlockSpec(memory_space=pltpu.VMEM)
SMEM = pl.BlockSpec(memory_space=pltpu.SMEM)


def on_device(groups, tokens, proj, state, step_rates, d_out):
    rows, width = tokens.shape[2:]
    heads, _, dim, hid = state.shape[1:]
    owned = proj.shape[0]
    peers = groups
    span = CORES * rows
    spot = lax.axis_index("seq")
    core = lax.rem(spot, CORES)
    place = spot // CORES

    def to_mate(value):
        return lax.ppermute(
            value, "seq", [(i, (i // CORES) * CORES + (i + 1) % CORES) for i in range(groups * CORES)]
        )

    def along(value, hop):
        return lax.ppermute(
            value,
            "seq",
            [(i, ((i // CORES + hop) % groups) * CORES + i % CORES) for i in range(groups * CORES)],
        )

    hops = range(1, groups)
    flat = lax.axis_index("fsdp")
    side = lax.rem(flat, 2)
    devices = lax.axis_size("fsdp")
    planes = [list(range(first, devices, 2)) for first in range(2)]
    plane = devices // 2

    def across(value):
        return lax.ppermute(value, "fsdp", [(i, i + 1 - 2 * (i % 2)) for i in range(devices)])

    def mine(value):
        half = value.shape[-1] // CORES
        return jnp.where(core == 0, value[..., :half], value[..., half:])

    proj_mine = mine(proj).reshape(owned, 3 * dim)
    proj_pair = across(proj_mine)
    both = jnp.where(
        side == 0,
        jnp.concatenate([proj_mine, proj_pair], axis=0),
        jnp.concatenate([proj_pair, proj_mine], axis=0),
    )
    own_state = jnp.where(core == 0, state[0, 0], state[0, 1])

    tok = tokens[0]
    half_rows = rows // 2
    rate_high = step_rates[0].astype(BF)
    rate_low = (step_rates[0] - rate_high.astype(F32)).astype(BF)
    rate_line = jnp.concatenate([rate_high[0], rate_high[1], rate_low[0], rate_low[1]])
    rate_rows = jnp.broadcast_to(jnp.tile(rate_line, width // (4 * rows)), (16, width))
    packed = jnp.concatenate([tok[0], rate_rows], axis=0)
    local_mate = to_mate(jnp.concatenate([packed, tok[1]], axis=0))
    both, local_mate = lax.optimization_barrier((both, local_mate))
    whole = lax.all_to_all(
        jnp.broadcast_to(both, (plane, 2 * owned, 3 * dim)),
        "fsdp",
        0,
        0,
        axis_index_groups=planes,
        tiled=True,
    ).reshape(devices * owned, 3 * dim)
    packed_mate = local_mate[: packed.shape[0]]
    tok1_mate = local_mate[packed.shape[0] :]
    head_dim = d_out.shape[-1] // CORES
    cot = mine(d_out[0])
    cot_mate = to_mate(jnp.where(core == 0, d_out[0, :, :, head_dim:], d_out[0, :, :, :head_dim]))
    cot0, cot0_mate = cot[0], cot_mate[0]
    ahead = along(packed, 1)
    behind = along(packed, groups - 1)
    far_low = along(ahead[:, : width // 2], 1)
    far_high = along(behind[:, width // 2 :], groups - 1)
    pieces = [packed, packed_mate, ahead, to_mate(ahead), behind, to_mate(behind)]
    pieces += [far_low, far_high, to_mate(far_low), to_mate(far_high)]

    second = jnp.concatenate([tok[1], tok1_mate], axis=0)
    query1 = jnp.dot(second, whole[:, :dim], preferred_element_type=F32).astype(BF)
    late_in = jnp.concatenate([query1, jnp.concatenate([cot[1], cot_mate[1]], axis=0)], axis=1)
    late_in, far_low, far_high = lax.optimization_barrier((late_in, far_low, far_high))
    late_ahead = along(late_in, 1)
    late_behind = along(late_in, groups - 1)
    lates = [late_in, late_ahead, late_behind]
    lates += [along(late_ahead[:, :dim], 1), along(late_behind[:, dim:], groups - 1)]

    shape = jax.ShapeDtypeStruct
    params = pltpu.CompilerParams(vmem_limit_bytes=56 * 2**20)
    early, dq0 = pl.pallas_call(
        early_kernel,
        out_shape=(shape((3, dim, hid), F32), shape((span, dim), BF)),
        in_specs=[VMEM] * 6,
        out_specs=(VMEM,) * 2,
        compiler_params=params,
        cost_estimate=pl.CostEstimate(flops=4*10**9, bytes_accessed=6 * 2**20, transcendentals=0),
        name="early",
    )(whole, own_state, tok[0], packed_mate[:rows], cot0, cot0_mate)

    spots = jnp.stack([place, core]).astype(jnp.int32)
    next16, kv, rates = pl.pallas_call(
        partial(update_kernel, groups, rows),
        out_shape=(
            shape((3, dim, hid), BF),
            shape((span, 2 * dim), BF),
            shape((groups * span, 128), F32),
        ),
        in_specs=[SMEM] + [VMEM] * (2 * groups + 4),
        out_specs=(VMEM,) * 3,
        scratch_shapes=[
            pltpu.VMEM((groups * span, 2 * dim), BF),
            pltpu.VMEM((3, dim, hid), BF),
            pltpu.VMEM((3, dim, hid), F32),
        ],
        compiler_params=params,
        cost_estimate=pl.CostEstimate(flops=9*10**9, bytes_accessed=6 * 2**20, transcendentals=0),
        name="update",
    )(core.reshape(1).astype(jnp.int32), *pieces, whole, own_state)

    share = dim // groups
    carried, shares, dproj, grads0, grads1 = pl.pallas_call(
        partial(late_kernel, groups, rows),
        out_shape=(
            shape((3, share, hid), F32),
            shape((groups, 3, share, hid), BF),
            shape((width, 3 * dim), BF),
            shape((span, 3 * dim), BF),
            shape((span, dim), BF),
        ),
        in_specs=[SMEM] + [VMEM] * (groups + 11),
        out_specs=(VMEM,) * 5,
        scratch_shapes=[
            pltpu.VMEM((3, dim, hid), BF),
            pltpu.VMEM((3, dim, hid), BF),
            pltpu.VMEM((3, dim, hid), F32),
        ],
        compiler_params=params,
        cost_estimate=pl.CostEstimate(flops=11*10**9, bytes_accessed=6 * 2**20, transcendentals=0),
        name="late",
    )(
        spots,
        *lates,
        next16,
        own_state,
        rates,
        kv,
        early,
        dq0,
        packed,
        packed_mate,
        tok[1],
        tok1_mate,
    )

    swapped = lax.all_to_all(
        dproj.reshape(plane, 2 * owned, 3 * dim),
        "fsdp",
        0,
        0,
        axis_index_groups=planes,
        tiled=True,
    )
    pair_sum = jnp.sum(swapped.astype(F32), axis=0)
    pair_keep = jnp.where(side == 0, pair_sum[:owned], pair_sum[owned:])
    pair_give = jnp.where(side == 0, pair_sum[owned:], pair_sum[:owned]).astype(BF)
    owner = (pair_keep + across(pair_give).astype(F32)).astype(BF)
    owner_all = owner.astype(F32)
    for hop in hops:
        owner_all = owner_all + along(owner, hop).astype(F32)
    owner_mate = to_mate(owner_all)
    owner_all = owner_all.reshape(owned, 3, dim)
    owner_mate = owner_mate.reshape(owned, 3, dim)
    d_proj = jnp.where(
        core == 0,
        jnp.concatenate([owner_all, owner_mate], axis=-1),
        jnp.concatenate([owner_mate, owner_all], axis=-1),
    )

    summed = carried + shares[0].astype(F32)
    for hop in hops:
        summed = summed + along(shares[hop], hop).astype(F32)
    half = share // CORES
    keep = jnp.where(core == 0, summed[:, :half], summed[:, half:])
    give = jnp.where(core == 0, summed[:, half:], summed[:, :half])
    got = to_mate(give)
    d_state = jnp.where(core == 0, jnp.stack([keep, got]), jnp.stack([got, keep]))[None]

    part0 = lax.dot_general(
        grads0, whole, (((1,), (1,)), ((), ())), preferred_element_type=F32
    )
    part1 = lax.dot_general(
        grads1, whole[:, :dim], (((1,), (1,)), ((), ())), preferred_element_type=F32
    )
    part = jnp.stack([part0, part1])
    from_mate = to_mate(part[:, rows:].astype(BF))
    d_tokens = (part[:, :rows] + from_mate.astype(F32)).astype(BF)[None]
    return (d_tokens, d_state, d_proj)


def solution(mesh):
    groups = mesh.shape["seq"] // CORES
    placed = (
        P("fsdp", None, "seq", None),
        P("fsdp", None, None),
        P("fsdp", None, None, None, None),
        P("fsdp", None, "seq"),
        P("fsdp", None, "seq", None),
    )
    return jax.shard_map(
        partial(on_device, groups),
        mesh=mesh,
        in_specs=placed,
        out_specs=(
            P("fsdp", None, "seq", None),
            P("fsdp", None, None, "seq", None),
            P("fsdp", None, None),
        ),
        check_vma=False,
    )
```

```python
from functools import partial

import jax
import jax.numpy as jnp
from jax import lax
from jax.experimental import pallas as pl
from jax.experimental.pallas import tpu as pltpu
from jax.sharding import PartitionSpec as P

EPS = 1e-06
BF = jnp.bfloat16
F32 = jnp.float32
CORES = 2


def dot_nn(a, b):
    return lax.dot_general(a, b, (((1,), (0,)), ((), ())), preferred_element_type=F32)


def dot_nt(a, b):
    return lax.dot_general(a, b, (((1,), (1,)), ((), ())), preferred_element_type=F32)


def dot_tn(a, b):
    return lax.dot_general(a, b, (((0,), (0,)), ((), ())), preferred_element_type=F32)


def inverse_rms(values):
    return lax.rsqrt(jnp.mean(values * values, axis=-1, keepdims=True) + EPS)


def unit_pull(grad, unit, scale):
    return scale * (grad - unit * jnp.mean(grad * unit, axis=-1, keepdims=True))


def as_column(row):
    count = row.shape[1]
    eye = lax.broadcasted_iota(jnp.int32, (count, count), 0) == lax.broadcasted_iota(
        jnp.int32, (count, count), 1
    )
    return jnp.sum(jnp.where(eye, row, 0.0), axis=1, keepdims=True)


def hidden_parts(unit, cot, weights):
    gate = dot_nn(unit, weights[0])
    up = dot_nn(unit, weights[1])
    back = dot_nn(cot, weights[2])
    sig = 0.5 * jnp.tanh(0.5 * gate) + 0.5
    act = gate * sig
    slope = sig + act * (1.0 - sig)
    return gate, up, back, sig, act, slope


def weight_terms(unit, cot, weights):
    gate, up, back, sig, act, slope = hidden_parts(unit, cot, weights)
    d_up = (back * act).astype(BF)
    d_gate = (back * up * slope).astype(BF)
    hidden = (act * up).astype(BF)
    return d_gate, d_up, hidden


def piece_refs(refs, count):
    pieces = []
    for ref in refs[: 2 * (count - 1)]:
        half = ref.shape[1] // 2
        pieces.append((ref.at[:, :half], ref.at[:, half:]))
    for low, high in zip(refs[2 * (count - 1) :: 2], refs[2 * (count - 1) + 1 :: 2]):
        pieces.append((low, high))
    return pieces


def piece_rate(piece, rows, head):
    low, width = piece[0], rows
    row = rows
    line = low[row : row + 16, :].astype(F32)
    halves = []
    for level in range(2):
        pick = line[0:1, level * CORES * width : (level * CORES + 1) * width]
        rest = line[0:1, (level * CORES + 1) * width : (level + 1) * CORES * width]
        halves.append(jnp.where(head == 0, pick, rest))
    return as_column(halves[0] + halves[1])


def early_kernel(whole, state, tok, tok_mate, cot, cot_mate, early_ref, dq_ref):
    dim = state.shape[1]
    w1, w3, w2 = (state[part].astype(BF) for part in range(3))
    own = jnp.concatenate([tok[...], tok_mate[...]], axis=0)
    query = dot_nn(own, whole[:, :dim]).astype(BF).astype(F32)
    scale = inverse_rms(query)
    unit = query * scale
    unit16 = unit.astype(BF)
    cots = jnp.concatenate([cot[...], cot_mate[...]], axis=0)
    d_gate, d_up, hidden = weight_terms(unit16, cots, (w1, w3, w2))
    early_ref[0] = dot_tn(unit16, d_gate)
    early_ref[1] = dot_tn(unit16, d_up)
    early_ref[2] = dot_tn(cots, hidden)
    pulled = dot_nt(d_gate, w1) + dot_nt(d_up, w3)
    dq_ref[...] = unit_pull(pulled, unit, scale).astype(BF)


def update_kernel(count, rows, head_ref, *refs):
    refs = list(refs)
    pieces = piece_refs(refs[: 2 * count + 2], count)
    whole, state, next_ref, kv_ref, rate_ref, keys, rate_all, w16, total = refs[2 * count + 2 :]
    dim = state.shape[1]
    half = whole.shape[0] // 2
    head = head_ref[0]
    for part in range(3):
        w16[part] = state[part].astype(BF)
        total[part] = state[part]
    group = len(pieces) // 2
    for first in range(0, len(pieces), group):
        some = pieces[first : first + group]
        low = jnp.concatenate([piece[0][:rows, :] for piece in some], axis=0)
        high = jnp.concatenate([piece[1][:rows, :] for piece in some], axis=0)
        out = dot_nn(low, whole[:half, dim:]) + dot_nn(high, whole[half:, dim:])
        keys[first * rows : (first + group) * rows, :] = out.astype(BF)
    for index, piece in enumerate(pieces):
        rate_all[index * rows : (index + 1) * rows, :] = jnp.broadcast_to(
            piece_rate(piece, rows, head), (rows, rate_all.shape[1])
        )
    span = CORES * rows
    kv_ref[...] = keys[:span, :]
    rate_ref[...] = rate_all[:span, :]
    block_rows = group * rows

    def step(block, carry):
        at = pl.ds(pl.multiple_of(block * block_rows, block_rows), block_rows)
        pair = keys[at, :].astype(F32)
        rate = rate_all[at, :1]
        key = pair[:, :dim]
        unit16 = (key * inverse_rms(key)).astype(BF)
        cot = (pair[:, dim:] * rate).astype(BF)
        d_gate, d_up, hidden = weight_terms(unit16, cot, (w16[0], w16[1], w16[2]))
        total[0] += dot_tn(unit16, d_gate)
        total[1] += dot_tn(unit16, d_up)
        total[2] += dot_tn(cot, hidden)
        return carry

    lax.fori_loop(0, 2, step, 0)
    for part in range(3):
        next_ref[part] = total[part].astype(BF)


def late_kernel(count, rows, place, *refs):
    refs = list(refs)
    dim = refs[count + 2].shape[1]
    queries = [ref.at[:, :dim] for ref in refs[: count - 1]] + [refs[count - 1]]
    cots = [ref.at[:, dim:] for ref in refs[: count - 1]] + [refs[count]]
    (next_w, state, rates, kv, early, dq0, tok0, tok0_mate, tok1, tok1_mate) = refs[
        count + 1 : count + 11
    ]
    (own_ref, share_ref, dproj_ref, g0_ref, g1_ref) = refs[count + 11 : count + 16]
    w16, c16, total = refs[count + 16 :]
    span, dim = kv.shape[0], state.shape[1]
    share = dim // count
    for part in range(3):
        w16[part] = state[part].astype(BF)
    late = (next_w[0], next_w[1], next_w[2])
    for block in range(2):
        size = count // 2
        picks = range(block * size, (block + 1) * size)
        query = jnp.concatenate([queries[i][...] for i in picks], axis=0).astype(F32)
        scale = inverse_rms(query)
        unit = query * scale
        unit16 = unit.astype(BF)
        cot = jnp.concatenate([cots[i][...] for i in picks], axis=0)
        d_gate, d_up, hidden = weight_terms(unit16, cot, late)
        terms = (dot_tn(unit16, d_gate), dot_tn(unit16, d_up), dot_tn(cot, hidden))
        for part in range(3):
            total[part] = terms[part] if block == 0 else total[part] + terms[part]
        if block == 0:
            pulled = dot_nt(d_gate[:span], late[0]) + dot_nt(d_up[:span], late[1])
            g1_ref[...] = unit_pull(pulled, unit[:span], scale[:span]).astype(BF)
    for part in range(3):
        c16[part] = total[part].astype(BF)
    start = pl.multiple_of(place[0] * share, share)
    for part in range(3):
        own_ref[part] = total[part, pl.ds(start, share), :]

    pair = kv[...].astype(F32)
    key, value = pair[:, :dim], pair[:, dim:]
    rate = rates[:span, :1]
    scale = inverse_rms(key)
    unit = key * scale
    unit16 = unit.astype(BF)
    cot = (value * rate).astype(BF)
    gate, up, back, sig, act, slope = hidden_parts(unit16, cot, (w16[0], w16[1], w16[2]))
    curve = sig * (1.0 - sig) * (2.0 + gate * (1.0 - 2.0 * sig))
    gate_dot = dot_nn(unit16, c16[0])
    up_dot = dot_nn(unit16, c16[1])
    back_dot = dot_nn(cot, c16[2])
    d_up1 = (back * act).astype(BF)
    d_gate1 = (back * up * slope).astype(BF)
    hidden = (act * up).astype(BF)
    slope_dot = slope * gate_dot
    hidden_dot = (slope_dot * up + act * up_dot).astype(BF)
    d_gate = (back * (curve * gate_dot * up + slope * up_dot) + back_dot * slope * up).astype(BF)
    d_up = (back * slope_dot + back_dot * act).astype(BF)
    d_value = rate * (dot_nt(hidden_dot, w16[2]) + dot_nt(hidden, c16[2]))
    d_unit = (
        dot_nt(d_gate, w16[0])
        + dot_nt(d_up, w16[1])
        + dot_nt(d_gate1, c16[0])
        + dot_nt(d_up1, c16[1])
    )
    g0_ref[:, :dim] = dq0[...]
    g0_ref[:, dim : 2 * dim] = unit_pull(d_unit, unit, scale).astype(BF)
    g0_ref[:, 2 * dim :] = d_value.astype(BF)
    total[0] = early[0] + dot_tn(unit16, d_gate)
    total[1] = early[1] + dot_tn(unit16, d_up)
    total[2] = early[2] + dot_tn(cot, hidden_dot)
    for other in range(count):
        at = lax.rem(place[0] + other, count)
        at = pl.multiple_of(at * share, share)
        for part in range(3):
            share_ref[other, part] = total[part, pl.ds(at, share), :].astype(BF)

    width = tok0.shape[1]
    columns = 256

    def project(step, carry):
        at = pl.ds(pl.multiple_of(step * columns, columns), columns)
        first = jnp.concatenate([tok0[:rows, at], tok0_mate[:rows, at]], axis=0)
        second = jnp.concatenate([tok1[:, at], tok1_mate[:, at]], axis=0)
        out = dot_tn(first, g0_ref[...])
        extra = dot_tn(second, g1_ref[...])
        dproj_ref[at, :dim] = (out[:, :dim] + extra).astype(BF)
        dproj_ref[at, dim:] = out[:, dim:].astype(BF)
        return carry

    lax.fori_loop(0, width // columns, project, 0)


VMEM = pl.BlockSpec(memory_space=pltpu.VMEM)
SMEM = pl.BlockSpec(memory_space=pltpu.SMEM)


def on_device(groups, tokens, proj, state, step_rates, d_out):
    rows, width = tokens.shape[2:]
    heads, _, dim, hid = state.shape[1:]
    owned = proj.shape[0]
    peers = groups
    span = CORES * rows
    spot = lax.axis_index("seq")
    core = lax.rem(spot, CORES)
    place = spot // CORES

    def to_mate(value):
        return lax.ppermute(
            value, "seq", [(i, (i // CORES) * CORES + (i + 1) % CORES) for i in range(groups * CORES)]
        )

    def along(value, hop):
        return lax.ppermute(
            value,
            "seq",
            [(i, ((i // CORES + hop) % groups) * CORES + i % CORES) for i in range(groups * CORES)],
        )

    hops = range(1, groups)
    flat = lax.axis_index("fsdp")
    side = lax.rem(flat, 2)
    devices = lax.axis_size("fsdp")
    planes = [list(range(first, devices, 2)) for first in range(2)]
    plane = devices // 2

    def across(value):
        return lax.ppermute(value, "fsdp", [(i, i + 1 - 2 * (i % 2)) for i in range(devices)])

    def mine(value):
        half = value.shape[-1] // CORES
        return jnp.where(core == 0, value[..., :half], value[..., half:])

    proj_mine = mine(proj).reshape(owned, 3 * dim)
    proj_pair = across(proj_mine)
    both = jnp.where(
        side == 0,
        jnp.concatenate([proj_mine, proj_pair], axis=0),
        jnp.concatenate([proj_pair, proj_mine], axis=0),
    )
    own_state = jnp.where(core == 0, state[0, 0], state[0, 1])

    tok = tokens[0]
    half_rows = rows // 2
    rate_high = step_rates[0].astype(BF)
    rate_low = (step_rates[0] - rate_high.astype(F32)).astype(BF)
    rate_line = jnp.concatenate([rate_high[0], rate_high[1], rate_low[0], rate_low[1]])
    rate_rows = jnp.broadcast_to(jnp.tile(rate_line, width // (4 * rows)), (16, width))
    packed = jnp.concatenate([tok[0], rate_rows], axis=0)
    local_mate = to_mate(jnp.concatenate([packed, tok[1]], axis=0))
    both, local_mate = lax.optimization_barrier((both, local_mate))
    whole = lax.all_to_all(
        jnp.broadcast_to(both, (plane, 2 * owned, 3 * dim)),
        "fsdp",
        0,
        0,
        axis_index_groups=planes,
        tiled=True,
    ).reshape(devices * owned, 3 * dim)
    packed_mate = local_mate[: packed.shape[0]]
    tok1_mate = local_mate[packed.shape[0] :]
    head_dim = d_out.shape[-1] // CORES
    cot = mine(d_out[0])
    cot_mate = to_mate(jnp.where(core == 0, d_out[0, :, :, head_dim:], d_out[0, :, :, :head_dim]))
    cot0, cot0_mate = cot[0], cot_mate[0]
    ahead = along(packed, 1)
    behind = along(packed, groups - 1)
    far_low = along(ahead[:, : width // 2], 1)
    far_high = along(behind[:, width // 2 :], groups - 1)
    pieces = [packed, packed_mate, ahead, to_mate(ahead), behind, to_mate(behind)]
    pieces += [far_low, far_high, to_mate(far_low), to_mate(far_high)]

    second = jnp.concatenate([tok[1], tok1_mate], axis=0)
    query1 = jnp.dot(second, whole[:, :dim], preferred_element_type=F32).astype(BF)
    late_in = jnp.concatenate([query1, jnp.concatenate([cot[1], cot_mate[1]], axis=0)], axis=1)
    late_in, far_low, far_high = lax.optimization_barrier((late_in, far_low, far_high))
    late_ahead = along(late_in, 1)
    late_behind = along(late_in, groups - 1)
    lates = [late_in, late_ahead, late_behind]
    lates += [along(late_ahead[:, :dim], 1), along(late_behind[:, dim:], groups - 1)]

    shape = jax.ShapeDtypeStruct
    params = pltpu.CompilerParams(vmem_limit_bytes=56 * 2**20)
    early, dq0 = pl.pallas_call(
        early_kernel,
        out_shape=(shape((3, dim, hid), F32), shape((span, dim), BF)),
        in_specs=[VMEM] * 6,
        out_specs=(VMEM,) * 2,
        compiler_params=params,
        cost_estimate=pl.CostEstimate(flops=4*10**9, bytes_accessed=6 * 2**20, transcendentals=0),
        name="early",
    )(whole, own_state, tok[0], packed_mate[:rows], cot0, cot0_mate)

    spots = jnp.stack([place, core]).astype(jnp.int32)
    next16, kv, rates = pl.pallas_call(
        partial(update_kernel, groups, rows),
        out_shape=(
            shape((3, dim, hid), BF),
            shape((span, 2 * dim), BF),
            shape((span, 128), F32),
        ),
        in_specs=[SMEM] + [VMEM] * (2 * groups + 4),
        out_specs=(VMEM,) * 3,
        scratch_shapes=[
            pltpu.VMEM((groups * span, 2 * dim), BF),
            pltpu.VMEM((groups * span, 128), F32),
            pltpu.VMEM((3, dim, hid), BF),
            pltpu.VMEM((3, dim, hid), F32),
        ],
        compiler_params=params,
        cost_estimate=pl.CostEstimate(flops=9*10**9, bytes_accessed=6 * 2**20, transcendentals=0),
        name="update",
    )(core.reshape(1).astype(jnp.int32), *pieces, whole, own_state)

    share = dim // groups
    carried, shares, dproj, grads0, grads1 = pl.pallas_call(
        partial(late_kernel, groups, rows),
        out_shape=(
            shape((3, share, hid), F32),
            shape((groups, 3, share, hid), BF),
            shape((width, 3 * dim), BF),
            shape((span, 3 * dim), BF),
            shape((span, dim), BF),
        ),
        in_specs=[SMEM] + [VMEM] * (groups + 11),
        out_specs=(VMEM,) * 5,
        scratch_shapes=[
            pltpu.VMEM((3, dim, hid), BF),
            pltpu.VMEM((3, dim, hid), BF),
            pltpu.VMEM((3, dim, hid), F32),
        ],
        compiler_params=params,
        cost_estimate=pl.CostEstimate(flops=11*10**9, bytes_accessed=6 * 2**20, transcendentals=0),
        name="late",
    )(
        spots,
        *lates,
        next16,
        own_state,
        rates,
        kv,
        early,
        dq0,
        packed,
        packed_mate,
        tok[1],
        tok1_mate,
    )

    swapped = lax.all_to_all(
        dproj.reshape(plane, 2 * owned, 3 * dim),
        "fsdp",
        0,
        0,
        axis_index_groups=planes,
        tiled=True,
    )
    pair_sum = jnp.sum(swapped.astype(F32), axis=0)
    pair_keep = jnp.where(side == 0, pair_sum[:owned], pair_sum[owned:])
    pair_give = jnp.where(side == 0, pair_sum[owned:], pair_sum[:owned]).astype(BF)
    owner = (pair_keep + across(pair_give).astype(F32)).astype(BF)
    owner_all = owner.astype(F32)
    for hop in hops:
        owner_all = owner_all + along(owner, hop).astype(F32)
    summed = carried + shares[0].astype(F32)
    for hop in hops:
        summed = summed + along(shares[hop], hop).astype(F32)
    half = share // CORES
    keep = jnp.where(core == 0, summed[:, :half], summed[:, half:])
    give = jnp.where(core == 0, summed[:, half:], summed[:, :half])
    got = to_mate(give)
    d_state = jnp.where(core == 0, jnp.stack([keep, got]), jnp.stack([got, keep]))[None]

    part0 = lax.dot_general(
        grads0, whole, (((1,), (1,)), ((), ())), preferred_element_type=F32
    )
    part1 = lax.dot_general(
        grads1, whole[:, :dim], (((1,), (1,)), ((), ())), preferred_element_type=F32
    )
    part = jnp.stack([part0, part1])
    from_mate = to_mate(part[:, rows:].astype(BF))
    d_tokens = (part[:, :rows] + from_mate.astype(F32)).astype(BF)[None]
    owner_all, d_state, d_tokens = lax.optimization_barrier((owner_all, d_state, d_tokens))
    owner_mate = to_mate(owner_all)
    owner_all = owner_all.reshape(owned, 3, dim)
    owner_mate = owner_mate.reshape(owned, 3, dim)
    d_proj = jnp.where(
        core == 0,
        jnp.concatenate([owner_all, owner_mate], axis=-1),
        jnp.concatenate([owner_mate, owner_all], axis=-1),
    )

    return (d_tokens, d_state, d_proj)


def solution(mesh):
    groups = mesh.shape["seq"] // CORES
    placed = (
        P("fsdp", None, "seq", None),
        P("fsdp", None, None),
        P("fsdp", None, None, None, None),
        P("fsdp", None, "seq"),
        P("fsdp", None, "seq", None),
    )
    return jax.shard_map(
        partial(on_device, groups),
        mesh=mesh,
        in_specs=placed,
        out_specs=(
            P("fsdp", None, "seq", None),
            P("fsdp", None, None, "seq", None),
            P("fsdp", None, None),
        ),
        check_vma=False,
    )
```

```python
from functools import partial

import jax
import jax.numpy as jnp
from jax import lax
from jax.experimental import pallas as pl
from jax.experimental.pallas import tpu as pltpu
from jax.sharding import PartitionSpec as P

EPS = 1e-06
BF = jnp.bfloat16
F32 = jnp.float32
CORES = 2


def dot_nn(a, b):
    return lax.dot_general(a, b, (((1,), (0,)), ((), ())), preferred_element_type=F32)


def dot_nt(a, b):
    return lax.dot_general(a, b, (((1,), (1,)), ((), ())), preferred_element_type=F32)


def dot_tn(a, b):
    return lax.dot_general(a, b, (((0,), (0,)), ((), ())), preferred_element_type=F32)


def inverse_rms(values):
    return lax.rsqrt(jnp.mean(values * values, axis=-1, keepdims=True) + EPS)


def unit_pull(grad, unit, scale):
    return scale * (grad - unit * jnp.mean(grad * unit, axis=-1, keepdims=True))


def as_column(row):
    count = row.shape[1]
    eye = lax.broadcasted_iota(jnp.int32, (count, count), 0) == lax.broadcasted_iota(
        jnp.int32, (count, count), 1
    )
    return jnp.sum(jnp.where(eye, row, 0.0), axis=1, keepdims=True)


def hidden_parts(unit, cot, weights):
    gate = dot_nn(unit, weights[0])
    up = dot_nn(unit, weights[1])
    back = dot_nn(cot, weights[2])
    sig = 0.5 * jnp.tanh(0.5 * gate) + 0.5
    act = gate * sig
    slope = sig + act * (1.0 - sig)
    return gate, up, back, sig, act, slope


def weight_terms(unit, cot, weights):
    gate, up, back, sig, act, slope = hidden_parts(unit, cot, weights)
    d_up = (back * act).astype(BF)
    d_gate = (back * up * slope).astype(BF)
    hidden = (act * up).astype(BF)
    return d_gate, d_up, hidden


def piece_refs(refs, count):
    pieces = []
    for ref in refs[: 2 * (count - 1)]:
        half = ref.shape[1] // 2
        pieces.append((ref.at[:, :half], ref.at[:, half:]))
    for low, high in zip(refs[2 * (count - 1) :: 2], refs[2 * (count - 1) + 1 :: 2]):
        pieces.append((low, high))
    return pieces


def piece_rate(piece, rows, head):
    low, width = piece[0], rows
    row = rows
    line = low[row : row + 16, :].astype(F32)
    halves = []
    for level in range(2):
        pick = line[0:1, level * CORES * width : (level * CORES + 1) * width]
        rest = line[0:1, (level * CORES + 1) * width : (level + 1) * CORES * width]
        halves.append(jnp.where(head == 0, pick, rest))
    return as_column(halves[0] + halves[1])


def early_kernel(whole, state, tok, tok_mate, cot, cot_mate, early_ref, dq_ref):
    dim = state.shape[1]
    w1, w3, w2 = (state[part].astype(BF) for part in range(3))
    own = jnp.concatenate([tok[...], tok_mate[...]], axis=0)
    query = dot_nn(own, whole[:, :dim]).astype(BF).astype(F32)
    scale = inverse_rms(query)
    unit = query * scale
    unit16 = unit.astype(BF)
    cots = jnp.concatenate([cot[...], cot_mate[...]], axis=0)
    d_gate, d_up, hidden = weight_terms(unit16, cots, (w1, w3, w2))
    early_ref[0] = dot_tn(unit16, d_gate)
    early_ref[1] = dot_tn(unit16, d_up)
    early_ref[2] = dot_tn(cots, hidden)
    pulled = dot_nt(d_gate, w1) + dot_nt(d_up, w3)
    dq_ref[...] = unit_pull(pulled, unit, scale).astype(BF)


def update_kernel(count, rows, head_ref, *refs):
    refs = list(refs)
    pieces = piece_refs(refs[: 2 * count + 2], count)
    whole, state, next_ref, kv_ref, rate_ref, keys, rate_all, w16, total = refs[2 * count + 2 :]
    dim = state.shape[1]
    half = whole.shape[0] // 2
    head = head_ref[0]
    for part in range(3):
        w16[part] = state[part].astype(BF)
        total[part] = state[part]
    group = len(pieces) // 2
    for first in range(0, len(pieces), group):
        some = pieces[first : first + group]
        low = jnp.concatenate([piece[0][:rows, :] for piece in some], axis=0)
        high = jnp.concatenate([piece[1][:rows, :] for piece in some], axis=0)
        out = dot_nn(low, whole[:half, dim:]) + dot_nn(high, whole[half:, dim:])
        keys[first * rows : (first + group) * rows, :] = out.astype(BF)
    for index, piece in enumerate(pieces):
        rate_all[index * rows : (index + 1) * rows, :] = jnp.broadcast_to(
            piece_rate(piece, rows, head), (rows, rate_all.shape[1])
        )
    span = CORES * rows
    kv_ref[...] = keys[:span, :]
    rate_ref[...] = rate_all[:span, :]
    block_rows = group * rows

    def step(block, carry):
        at = pl.ds(pl.multiple_of(block * block_rows, block_rows), block_rows)
        pair = keys[at, :].astype(F32)
        rate = rate_all[at, :1]
        key = pair[:, :dim]
        unit16 = (key * inverse_rms(key)).astype(BF)
        cot = (pair[:, dim:] * rate).astype(BF)
        d_gate, d_up, hidden = weight_terms(unit16, cot, (w16[0], w16[1], w16[2]))
        total[0] += dot_tn(unit16, d_gate)
        total[1] += dot_tn(unit16, d_up)
        total[2] += dot_tn(cot, hidden)
        return carry

    lax.fori_loop(0, 2, step, 0)
    for part in range(3):
        next_ref[part] = total[part].astype(BF)


def late_kernel(count, rows, place, *refs):
    refs = list(refs)
    dim = refs[count + 2].shape[1]
    queries = [ref.at[:, :dim] for ref in refs[: count - 1]] + [refs[count - 1]]
    cots = [ref.at[:, dim:] for ref in refs[: count - 1]] + [refs[count]]
    (next_w, state, rates, kv, early, dq0, tok0, tok0_mate, tok1, tok1_mate) = refs[
        count + 1 : count + 11
    ]
    (own_ref, share_ref, dproj_ref, g0_ref, g1_ref) = refs[count + 11 : count + 16]
    w16, c16, total = refs[count + 16 :]
    span, dim = kv.shape[0], state.shape[1]
    share = dim // count
    for part in range(3):
        w16[part] = state[part].astype(BF)
    late = (next_w[0], next_w[1], next_w[2])
    for block in range(2):
        size = count // 2
        picks = range(block * size, (block + 1) * size)
        query = jnp.concatenate([queries[i][...] for i in picks], axis=0).astype(F32)
        scale = inverse_rms(query)
        unit = query * scale
        unit16 = unit.astype(BF)
        cot = jnp.concatenate([cots[i][...] for i in picks], axis=0)
        d_gate, d_up, hidden = weight_terms(unit16, cot, late)
        terms = (dot_tn(unit16, d_gate), dot_tn(unit16, d_up), dot_tn(cot, hidden))
        for part in range(3):
            total[part] = terms[part] if block == 0 else total[part] + terms[part]
        if block == 0:
            pulled = dot_nt(d_gate[:span], late[0]) + dot_nt(d_up[:span], late[1])
            g1_ref[...] = unit_pull(pulled, unit[:span], scale[:span]).astype(BF)
    for part in range(3):
        c16[part] = total[part].astype(BF)
    start = pl.multiple_of(place[0] * share, share)
    for part in range(3):
        own_ref[part] = total[part, pl.ds(start, share), :]

    pair = kv[...].astype(F32)
    key, value = pair[:, :dim], pair[:, dim:]
    rate = rates[:span, :1]
    scale = inverse_rms(key)
    unit = key * scale
    unit16 = unit.astype(BF)
    cot = (value * rate).astype(BF)
    gate, up, back, sig, act, slope = hidden_parts(unit16, cot, (w16[0], w16[1], w16[2]))
    curve = sig * (1.0 - sig) * (2.0 + gate * (1.0 - 2.0 * sig))
    gate_dot = dot_nn(unit16, c16[0])
    up_dot = dot_nn(unit16, c16[1])
    back_dot = dot_nn(cot, c16[2])
    d_up1 = (back * act).astype(BF)
    d_gate1 = (back * up * slope).astype(BF)
    hidden = (act * up).astype(BF)
    slope_dot = slope * gate_dot
    hidden_dot = (slope_dot * up + act * up_dot).astype(BF)
    d_gate = (back * (curve * gate_dot * up + slope * up_dot) + back_dot * slope * up).astype(BF)
    d_up = (back * slope_dot + back_dot * act).astype(BF)
    d_value = rate * (dot_nt(hidden_dot, w16[2]) + dot_nt(hidden, c16[2]))
    d_unit = (
        dot_nt(d_gate, w16[0])
        + dot_nt(d_up, w16[1])
        + dot_nt(d_gate1, c16[0])
        + dot_nt(d_up1, c16[1])
    )
    g0_ref[:, :dim] = dq0[...]
    g0_ref[:, dim : 2 * dim] = unit_pull(d_unit, unit, scale).astype(BF)
    g0_ref[:, 2 * dim :] = d_value.astype(BF)
    total[0] = early[0] + dot_tn(unit16, d_gate)
    total[1] = early[1] + dot_tn(unit16, d_up)
    total[2] = early[2] + dot_tn(cot, hidden_dot)
    for other in range(count):
        at = lax.rem(place[0] + other, count)
        at = pl.multiple_of(at * share, share)
        for part in range(3):
            share_ref[other, part] = total[part, pl.ds(at, share), :].astype(BF)

    width = tok0.shape[1]
    columns = 256

    def project(step, carry):
        at = pl.ds(pl.multiple_of(step * columns, columns), columns)
        first = jnp.concatenate([tok0[:rows, at], tok0_mate[:rows, at]], axis=0)
        second = jnp.concatenate([tok1[:, at], tok1_mate[:, at]], axis=0)
        out = dot_tn(first, g0_ref[...])
        extra = dot_tn(second, g1_ref[...])
        dproj_ref[at, :dim] = (out[:, :dim] + extra).astype(BF)
        dproj_ref[at, dim:] = out[:, dim:].astype(BF)
        return carry

    lax.fori_loop(0, width // columns, project, 0)


VMEM = pl.BlockSpec(memory_space=pltpu.VMEM)
SMEM = pl.BlockSpec(memory_space=pltpu.SMEM)


def on_device(groups, tokens, proj, state, step_rates, d_out):
    rows, width = tokens.shape[2:]
    heads, _, dim, hid = state.shape[1:]
    owned = proj.shape[0]
    peers = groups
    span = CORES * rows
    spot = lax.axis_index("seq")
    core = lax.rem(spot, CORES)
    place = spot // CORES

    def to_mate(value):
        return lax.ppermute(
            value, "seq", [(i, (i // CORES) * CORES + (i + 1) % CORES) for i in range(groups * CORES)]
        )

    def along(value, hop):
        return lax.ppermute(
            value,
            "seq",
            [(i, ((i // CORES + hop) % groups) * CORES + i % CORES) for i in range(groups * CORES)],
        )

    hops = range(1, groups)
    flat = lax.axis_index("fsdp")
    side = lax.rem(flat, 2)
    devices = lax.axis_size("fsdp")
    planes = [list(range(first, devices, 2)) for first in range(2)]
    plane = devices // 2

    def across(value):
        return lax.ppermute(value, "fsdp", [(i, i + 1 - 2 * (i % 2)) for i in range(devices)])

    def mine(value):
        half = value.shape[-1] // CORES
        return jnp.where(core == 0, value[..., :half], value[..., half:])

    proj_mine = mine(proj).reshape(owned, 3 * dim)
    proj_pair = across(proj_mine)
    both = jnp.where(
        side == 0,
        jnp.concatenate([proj_mine, proj_pair], axis=0),
        jnp.concatenate([proj_pair, proj_mine], axis=0),
    )

    tok = tokens[0]
    half_rows = rows // 2
    rate_high = step_rates[0].astype(BF)
    rate_low = (step_rates[0] - rate_high.astype(F32)).astype(BF)
    rate_line = jnp.concatenate([rate_high[0], rate_high[1], rate_low[0], rate_low[1]])
    rate_rows = jnp.broadcast_to(jnp.tile(rate_line, width // (4 * rows)), (16, width))
    packed = jnp.concatenate([tok[0], rate_rows], axis=0)
    local_mate = to_mate(jnp.concatenate([packed, tok[1]], axis=0))
    both, local_mate = lax.optimization_barrier((both, local_mate))
    whole = lax.all_to_all(
        jnp.broadcast_to(both, (plane, 2 * owned, 3 * dim)),
        "fsdp",
        0,
        0,
        axis_index_groups=planes,
        tiled=True,
    ).reshape(devices * owned, 3 * dim)
    packed_mate = local_mate[: packed.shape[0]]
    tok1_mate = local_mate[packed.shape[0] :]
    head_dim = d_out.shape[-1] // CORES
    cot = mine(d_out[0])
    cot_mate = to_mate(jnp.where(core == 0, d_out[0, :, :, head_dim:], d_out[0, :, :, :head_dim]))
    cot0, cot0_mate = cot[0], cot_mate[0]
    ahead = along(packed, 1)
    behind = along(packed, groups - 1)
    far_low = along(ahead[:, : width // 2], 1)
    far_high = along(behind[:, width // 2 :], groups - 1)
    pieces = [packed, packed_mate, ahead, to_mate(ahead), behind, to_mate(behind)]
    pieces += [far_low, far_high, to_mate(far_low), to_mate(far_high)]

    state, ahead = lax.optimization_barrier((state, ahead))
    own_state = jnp.where(core == 0, state[0, 0], state[0, 1])
    second = jnp.concatenate([tok[1], tok1_mate], axis=0)
    query1 = jnp.dot(second, whole[:, :dim], preferred_element_type=F32).astype(BF)
    late_in = jnp.concatenate([query1, jnp.concatenate([cot[1], cot_mate[1]], axis=0)], axis=1)
    late_in, far_low, far_high = lax.optimization_barrier((late_in, far_low, far_high))
    late_ahead = along(late_in, 1)
    late_behind = along(late_in, groups - 1)
    lates = [late_in, late_ahead, late_behind]
    lates += [along(late_ahead[:, :dim], 1), along(late_behind[:, dim:], groups - 1)]

    shape = jax.ShapeDtypeStruct
    params = pltpu.CompilerParams(vmem_limit_bytes=56 * 2**20)
    early, dq0 = pl.pallas_call(
        early_kernel,
        out_shape=(shape((3, dim, hid), F32), shape((span, dim), BF)),
        in_specs=[VMEM] * 6,
        out_specs=(VMEM,) * 2,
        compiler_params=params,
        cost_estimate=pl.CostEstimate(flops=4*10**9, bytes_accessed=6 * 2**20, transcendentals=0),
        name="early",
    )(whole, own_state, tok[0], packed_mate[:rows], cot0, cot0_mate)

    spots = jnp.stack([place, core]).astype(jnp.int32)
    next16, kv, rates = pl.pallas_call(
        partial(update_kernel, groups, rows),
        out_shape=(
            shape((3, dim, hid), BF),
            shape((span, 2 * dim), BF),
            shape((span, 128), F32),
        ),
        in_specs=[SMEM] + [VMEM] * (2 * groups + 4),
        out_specs=(VMEM,) * 3,
        scratch_shapes=[
            pltpu.VMEM((groups * span, 2 * dim), BF),
            pltpu.VMEM((groups * span, 128), F32),
            pltpu.VMEM((3, dim, hid), BF),
            pltpu.VMEM((3, dim, hid), F32),
        ],
        compiler_params=params,
        cost_estimate=pl.CostEstimate(flops=9*10**9, bytes_accessed=6 * 2**20, transcendentals=0),
        name="update",
    )(core.reshape(1).astype(jnp.int32), *pieces, whole, own_state)

    share = dim // groups
    carried, shares, dproj, grads0, grads1 = pl.pallas_call(
        partial(late_kernel, groups, rows),
        out_shape=(
            shape((3, share, hid), F32),
            shape((groups, 3, share, hid), BF),
            shape((width, 3 * dim), BF),
            shape((span, 3 * dim), BF),
            shape((span, dim), BF),
        ),
        in_specs=[SMEM] + [VMEM] * (groups + 11),
        out_specs=(VMEM,) * 5,
        scratch_shapes=[
            pltpu.VMEM((3, dim, hid), BF),
            pltpu.VMEM((3, dim, hid), BF),
            pltpu.VMEM((3, dim, hid), F32),
        ],
        compiler_params=params,
        cost_estimate=pl.CostEstimate(flops=11*10**9, bytes_accessed=6 * 2**20, transcendentals=0),
        name="late",
    )(
        spots,
        *lates,
        next16,
        own_state,
        rates,
        kv,
        early,
        dq0,
        packed,
        packed_mate,
        tok[1],
        tok1_mate,
    )

    swapped = lax.all_to_all(
        dproj.reshape(plane, 2 * owned, 3 * dim),
        "fsdp",
        0,
        0,
        axis_index_groups=planes,
        tiled=True,
    )
    pair_sum = jnp.sum(swapped.astype(F32), axis=0)
    pair_keep = jnp.where(side == 0, pair_sum[:owned], pair_sum[owned:])
    pair_give = jnp.where(side == 0, pair_sum[owned:], pair_sum[:owned]).astype(BF)
    owner = (pair_keep + across(pair_give).astype(F32)).astype(BF)
    owner_all = owner.astype(F32)
    for hop in hops:
        owner_all = owner_all + along(owner, hop).astype(F32)
    summed = carried + shares[0].astype(F32)
    for hop in hops:
        summed = summed + along(shares[hop], hop).astype(F32)
    half = share // CORES
    keep = jnp.where(core == 0, summed[:, :half], summed[:, half:])
    give = jnp.where(core == 0, summed[:, half:], summed[:, :half])
    got = to_mate(give)
    d_state = jnp.where(core == 0, jnp.stack([keep, got]), jnp.stack([got, keep]))[None]

    part0 = lax.dot_general(
        grads0, whole, (((1,), (1,)), ((), ())), preferred_element_type=F32
    )
    part1 = lax.dot_general(
        grads1, whole[:, :dim], (((1,), (1,)), ((), ())), preferred_element_type=F32
    )
    part = jnp.stack([part0, part1])
    from_mate = to_mate(part[:, rows:].astype(BF))
    d_tokens = (part[:, :rows] + from_mate.astype(F32)).astype(BF)[None]
    owner_all, d_state, d_tokens = lax.optimization_barrier((owner_all, d_state, d_tokens))
    owner_mate = to_mate(owner_all)
    owner_all = owner_all.reshape(owned, 3, dim)
    owner_mate = owner_mate.reshape(owned, 3, dim)
    d_proj = jnp.where(
        core == 0,
        jnp.concatenate([owner_all, owner_mate], axis=-1),
        jnp.concatenate([owner_mate, owner_all], axis=-1),
    )

    return (d_tokens, d_state, d_proj)


def solution(mesh):
    groups = mesh.shape["seq"] // CORES
    placed = (
        P("fsdp", None, "seq", None),
        P("fsdp", None, None),
        P("fsdp", None, None, None, None),
        P("fsdp", None, "seq"),
        P("fsdp", None, "seq", None),
    )
    return jax.shard_map(
        partial(on_device, groups),
        mesh=mesh,
        in_specs=placed,
        out_specs=(
            P("fsdp", None, "seq", None),
            P("fsdp", None, None, "seq", None),
            P("fsdp", None, None),
        ),
        check_vma=False,
    )
```
